32 devices in a mesh: bra: 8 (over z, y), ket: 4 (over x, core).
Axes of the slice: x: 2, y: 2, z: 4, core: 2. Of those that a mesh axis runs over, the one named last changes fastest.
Arguments:
- quartet_tasks: int32 [8, 4, 512, 4], P('bra', 'ket'), may hold values from 0 to 191, as said below
- factors: bfloat16 [192, 16, 128], replicated, may hold values from -4.5 to 4.5
- density: bfloat16 [192, 48, 4, 256], P('bra', None, 'ket'), may hold values from -6 to 6
Outputs:
- fock_matrix: float32 [192, 48, 4, 256], P('bra', None, 'ket')
The draws below stay inside these ranges and needn't reach their ends.
Inputs may be any that keep to these rules, and one draw needn't show every extreme that they name: `quartet_tasks`: entries are shell numbers. On the device with bra index b and ket index k, every task's i lies among b * 24 to (b + 1) * 24 - 1 and its d has d % 4 == k. Within each half of a device's task list (the first 256 tasks and the rest), the shells c and j of all its tasks name row blocks of one bra index at most 192 times and share one remainder mod 4 at most 160 times; both bounds are reached in each half of every device's list, by the same bra index and the same remainder in both halves.
All inputs are finite; a program needn't handle non-finite values.
Results may differ from the reference program's by a relative error of at most 0.0066.
Values may be sent and summed in bfloat16 or wider, within the bound.
A program may use at most 64 MiB of HBM per device.

```python
import jax
import jax.numpy as jnp
from jax import lax

FUNCS = 16
RANK = 128
BLK = 6
TASKS = 512
KETS = 4
NBLK = 192
ROWB = 24
COLB = 48
HALFB = 192
HALFK = 160
N_BRA = 8
N_KET = 4


def owner_list(key, forced, count_of_owners, capacity, item_count):
    second_key, third_key = jax.random.split(key, 2)
    slot_ids = jnp.arange(count_of_owners * capacity, dtype=jnp.int32)
    shuffled = jax.random.permutation(second_key, count_of_owners * capacity).astype(jnp.int32)
    ranking = jnp.argsort(shuffled, stable=True).astype(jnp.int32)
    scores = jnp.where(slot_ids // capacity == forced, slot_ids - count_of_owners * capacity, ranking)
    chosen = jnp.argsort(scores, stable=True)[:item_count].astype(jnp.int32)
    owner_ids = chosen // capacity
    mixing = jax.random.permutation(third_key, item_count)
    return owner_ids[mixing]


def draw_quartet_tasks(key, part):

    def one_device(device):
        device_key = jax.random.fold_in(key, device)
        bra_index = device // N_KET
        ket_index = device % N_KET
        forced_bra = jax.random.randint(jax.random.fold_in(device_key, 60), (), 0, N_BRA)
        forced_ket = jax.random.randint(jax.random.fold_in(device_key, 70), (), 0, N_KET)
        bra_owners = jnp.concatenate([owner_list(jax.random.fold_in(device_key, 10 + portion), forced_bra, N_BRA, HALFB, TASKS) for portion in range(2)])
        ket_owners = jnp.concatenate([owner_list(jax.random.fold_in(device_key, 20 + portion), forced_ket, N_KET, HALFK, TASKS) for portion in range(2)])
        inner = jax.random.randint(jax.random.fold_in(device_key, 30), (2 * TASKS,), 0, BLK)
        shells = bra_owners * ROWB + inner * N_KET + ket_owners
        shell_i = bra_index * ROWB + jax.random.randint(jax.random.fold_in(device_key, 40), (TASKS,), 0, ROWB)
        shell_d = jax.random.randint(jax.random.fold_in(device_key, 50), (TASKS,), 0, COLB) * N_KET + ket_index
        paired = shells.reshape(TASKS, 2)
        return jnp.stack([shell_i, paired[:, 1], paired[:, 0], shell_d], axis=1).astype(jnp.int32)
    devices = jnp.arange(N_BRA * N_KET, dtype=jnp.int32)
    return jax.vmap(one_device)(devices).reshape(N_BRA, N_KET, TASKS, 4)


def steps_of(rng, extent, pieces, smallest, top_value):
    def one(axis_at, shards_of):
        heights = jax.random.uniform(jax.random.fold_in(jax.random.fold_in(rng, 6), axis_at), (shards_of,), jnp.float32, smallest / len(pieces), top_value / len(pieces))
        return jnp.repeat(jnp.exp(heights), extent[axis_at] // shards_of).reshape((-1,) + (1,) * (len(extent) - axis_at - 1))

    level = one(*pieces[0])
    for cut in pieces[1:]:
        level = level * one(*cut)
    return level


def centred(stream_key, shape, deviation, limit, pieces=(), held_as=jnp.bfloat16):
    factor_of = steps_of(stream_key, shape, pieces, -0.22, 0.18) if pieces else 1.0
    drawn = jax.random.normal(stream_key, shape, jnp.float32) * deviation * factor_of
    return jnp.minimum(jnp.maximum(drawn, -limit), limit).astype(held_as)


def setup_inputs(seed: int = 0) -> dict:
    seeds = jax.random.split(jax.random.key(seed), 4)
    return {
        "quartet_tasks": draw_quartet_tasks(jax.random.fold_in(seeds[3], 71), 0),
        "factors": centred(seeds[1], (NBLK, FUNCS, RANK), 0.75, 4.5),
        "density": centred(seeds[2], (NBLK, COLB, KETS, FUNCS * FUNCS), 1.0, 6.0, ((0, 8), (2, 4))),
    }


tile_scale = 0.0625

def pair_vectors(left_shell, right_shell):
    shell_count, basis_functions, terms = left_shell.shape
    joined = left_shell[:, :, None, :].astype(jnp.float32) * right_shell[:, None, :, :].astype(jnp.float32)
    return joined.reshape(shell_count, basis_functions * basis_functions, terms).astype(jnp.bfloat16)

def quartet_terms(factors, task_group, dens_cd, density_block_jd):
    group_member_count = task_group.shape[0]
    basis_functions = factors.shape[1]
    bra_vec = pair_vectors(factors[task_group[:, 0]], factors[task_group[:, 1]])
    ket_vec = pair_vectors(factors[task_group[:, 2]], factors[task_group[:, 3]])
    raw_products = jnp.einsum('tpr,tqr->tpq', bra_vec.astype(jnp.float32), ket_vec.astype(jnp.float32))
    integral_tile = (tile_scale * raw_products * lax.rsqrt(1.0 + raw_products * raw_products)).astype(jnp.bfloat16)
    coulomb = jnp.einsum('tpq,tq->tp', integral_tile.astype(jnp.float32), dens_cd.astype(jnp.float32))
    reshaped_tile = integral_tile.reshape(group_member_count, basis_functions, basis_functions, basis_functions, basis_functions).astype(jnp.float32)
    exchange_contribution = jnp.einsum('kwzmp,kzp->kwm', reshaped_tile, density_block_jd.reshape(group_member_count, basis_functions, basis_functions).astype(jnp.float32))
    return (coulomb, exchange_contribution.reshape(group_member_count, basis_functions * basis_functions))

def reference(quartet_tasks, factors, density):
    quartets = quartet_tasks.reshape(-1, 4)
    block_size = density.shape[3]

    def block_step(task_group):
        shell_j = task_group[:, 1]
        shell_c = task_group[:, 2]
        shell_d = task_group[:, 3]
        dens_cd = density[shell_c, shell_d // KETS, shell_d % KETS]
        density_block_jd = density[shell_j, shell_d // KETS, shell_d % KETS]
        return quartet_terms(factors, task_group, dens_cd, density_block_jd)
    coulomb, exchange_contribution = lax.map(block_step, quartets.reshape(-1, 32, 4))
    coulomb = coulomb.reshape(-1, block_size)
    exchange_contribution = exchange_contribution.reshape(-1, block_size)
    fock_matrix = jnp.zeros(density.shape, jnp.float32)
    fock_matrix = fock_matrix.at[quartets[:, 0], quartets[:, 1] // KETS, quartets[:, 1] % KETS].add(coulomb)
    fock_matrix = fock_matrix.at[quartets[:, 0], quartets[:, 2] // KETS, quartets[:, 2] % KETS].add(-0.5 * exchange_contribution)
    return fock_matrix
```

```python
import functools

import jax
import jax.numpy as jnp
from jax import lax
from jax.experimental import pallas as pl
from jax.experimental.pallas import tpu as pltpu
from jax.sharding import PartitionSpec as P

tile_scale = 0.0625
NT = (((1,), (1,)), ((), ()))
NN = (((1,), (0,)), ((), ()))
VMEM = pl.BlockSpec(memory_space=pltpu.VMEM)
SMEM = pl.BlockSpec(memory_space=pltpu.SMEM)
PARAMS = pltpu.CompilerParams(vmem_limit_bytes=48 * 1024 * 1024)


def iota(shape, axis):
    return lax.broadcasted_iota(jnp.int32, shape, axis)


def dot(left, right, dims):
    return lax.dot_general(left, right, dims, preferred_element_type=jnp.float32)


def hot(mask):
    return jnp.where(mask, 1.0, 0.0).astype(jnp.bfloat16)


def plan_kernel(sides, bucket_refs, wanted_refs, slot_refs, asked_refs):
    items = bucket_refs[0].shape[1]
    upper = hot(iota((items, items), 0) <= iota((items, items), 1))
    for side, (buckets, capacity) in enumerate(sides):
        owner_id = iota((buckets, items), 0)
        marked = jnp.where(bucket_refs[side][...] == owner_id, 1.0, 0.0)
        counted = dot(marked.astype(jnp.bfloat16), upper, NN)
        offset = (owner_id * capacity - 1).astype(jnp.float32)
        slot = jnp.sum(marked * (counted + offset), axis=0, keepdims=True).astype(jnp.int32)
        slot_refs[side][...] = slot
        wanted = wanted_refs[side][...]
        which = iota((16, items), 0)
        high, low = wanted >> 6, wanted & 63
        values = jnp.where(which == 0, high, jnp.where(which == 1, low, 0))
        values = values.astype(jnp.float32).astype(jnp.bfloat16)
        width = 256

        def part(k, carry, side=side, slot=slot, values=values):
            first = pl.multiple_of(k * width, width)
            picked = hot(slot == iota((width, items), 0) + first)
            found = dot(values, picked, NT)
            asked_refs[side][:, pl.ds(first, width)] = (
                found[0:1] * 64.0 + found[1:2]
            ).astype(jnp.int32)
            return carry

        lax.fori_loop(0, buckets * capacity // width, part, 0)


def plan(buckets, wanted, sides):
    count = len(sides)
    items = buckets[0].shape[1]

    def kernel(*refs):
        plan_kernel(
            sides,
            refs[:count],
            refs[count : 2 * count],
            refs[2 * count : 3 * count],
            refs[3 * count :],
        )

    out = pl.pallas_call(
        kernel,
        out_shape=[jax.ShapeDtypeStruct((1, items), jnp.int32)] * count
        + [jax.ShapeDtypeStruct((1, b * c), jnp.int32) for b, c in sides],
        in_specs=[VMEM] * (2 * count),
        out_specs=[VMEM] * (2 * count),
        compiler_params=PARAMS,
        name="plan",
    )(*buckets, *wanted)
    return out[:count], out[count:]


def serve_kernel(ids_ref, table_ref, out_ref):
    rows = ids_ref.shape[1]
    blocks = table_ref.shape[0]
    spread = jnp.broadcast_to(ids_ref[...], (128, rows)).T
    spread = jnp.concatenate([spread] * (blocks // 128), axis=1)
    picked = hot(spread == iota((rows, blocks), 1))
    out_ref[...] = dot(picked, table_ref[...], NN).astype(jnp.bfloat16)


def serve(ids, table):
    wide = 256
    total = ids.shape[1]
    return pl.pallas_call(
        serve_kernel,
        grid=(total // wide,),
        out_shape=jax.ShapeDtypeStruct((total, table.shape[1]), jnp.bfloat16),
        in_specs=[
            pl.BlockSpec((1, wide), lambda k: (0, k)),
            pl.BlockSpec(table.shape, lambda k: (0, 0)),
        ],
        out_specs=pl.BlockSpec((wide, table.shape[1]), lambda k: (k, 0)),
        compiler_params=PARAMS,
        cost_estimate=pl.CostEstimate(
            flops=2 * total * table.shape[0] * table.shape[1],
            bytes_accessed=4 * total * table.shape[1],
            transcendentals=0,
        ),
        name="serve",
    )(ids, table)


def pair_rows(slow_ref, slow, fast):
    funcs = fast.shape[0]
    parts = []
    for at in range(funcs):
        row = jnp.broadcast_to(slow_ref[slow, at : at + 1, :], fast.shape).astype(jnp.bfloat16)
        parts.append(row * fast)
    return jnp.concatenate(parts, axis=0)


def task_kernel(
    tasks_ref, slots_ref, places_ref, fac_ref, got_ref, out_ref,
    fac32, got32, dens, spread, dens_cd, partial, coulomb, routed, unroll,
):
    shells, funcs, terms = fac_ref.shape
    size = funcs * funcs
    count = spread.shape[1]
    fac32[...] = fac_ref[...].astype(jnp.float32)
    got32[...] = got_ref[...].astype(jnp.float32)

    def gather(t, carry):
        for side in range(2):
            dens[side, pl.ds(t, 1), :] = got32[pl.ds(slots_ref[2 * t + side], 1), :]
        return carry

    lax.fori_loop(0, count, gather, 0, unroll=8)
    row, col = iota((size, size), 0), iota((size, size), 1)
    row_hi, row_lo, col_hi, col_lo = row // funcs, row % funcs, col // funcs, col % funcs
    swap = hot((row_hi == col_lo) & (row_lo == col_hi))
    dens_cd[...] = dot(dens[0].astype(jnp.bfloat16), swap, NN)
    dens_jd = dens[1].astype(jnp.bfloat16)

    def spread_one(f, carry):
        spread[f] = dot(dens_jd, hot((row_hi == col_lo) & (row_lo == f)), NN)
        return carry

    lax.fori_loop(0, funcs, spread_one, 0)

    def one_task(t):
        shell_i, shell_j = tasks_ref[4 * t], tasks_ref[4 * t + 1]
        shell_c, shell_d = tasks_ref[4 * t + 2], tasks_ref[4 * t + 3]
        ket = pair_rows(fac32, shell_d, fac_ref[shell_c])
        bra = pair_rows(fac32, shell_i, fac_ref[shell_j])
        raw = dot(ket, bra, NT)
        tile = raw * lax.rsqrt(1.0 + raw * raw)
        total = None
        for f in range(funcs):
            term = tile[f * funcs : (f + 1) * funcs] * spread[f, pl.ds(t, 1), :]
            total = term if total is None else total + term
        place = pl.ds(pl.multiple_of(t * funcs, funcs), funcs)
        for lane in range(size // 128):
            partial[lane, place, :] = total[:, lane * 128 : (lane + 1) * 128]
        weights = jnp.broadcast_to(dens_cd[pl.ds(t, 1), :], (16, size)).astype(jnp.bfloat16)
        summed = dot(weights, tile.astype(jnp.bfloat16), NN)
        coulomb[pl.ds(t, 1), :] = summed[0:1]

    def some_tasks(step, carry):
        for k in range(unroll):
            one_task(step * unroll + k)
        return carry

    lax.fori_loop(0, count // unroll, some_tasks, 0)

    dens[0] = coulomb[...] * tile_scale
    dens[1] = jnp.zeros((count, size), jnp.float32)

    def fold(e, carry):
        picked = pl.ds(e, count, stride=funcs)
        rows = [partial[lane, picked, :] for lane in range(size // 128)]
        rows = jnp.concatenate(rows, axis=1).astype(jnp.bfloat16)
        dens[1] += dot(rows, hot((row_hi == col_hi) & (col_lo == e)), NN)
        return carry

    lax.fori_loop(0, funcs, fold, 0)
    dens[1] = dens[1] * (-0.5 * tile_scale)
    routed[...] = jnp.zeros_like(routed)

    def route(t, carry):
        for side in range(2):
            routed[pl.ds(places_ref[2 * t + side], 1), :] = dens[side, pl.ds(t, 1), :]
        return carry

    lax.fori_loop(0, count, route, 0, unroll=8)
    out_ref[...] = routed[...].astype(jnp.bfloat16)


def run_tasks(tasks, slots, places, factors, got, out_rows, unroll):
    count = tasks.shape[0] // 4
    shells, funcs, terms = factors.shape
    size = funcs * funcs
    f32 = jnp.float32
    return pl.pallas_call(
        functools.partial(task_kernel, unroll=unroll),
        out_shape=jax.ShapeDtypeStruct((out_rows, size), jnp.bfloat16),
        in_specs=[SMEM, SMEM, SMEM, VMEM, VMEM],
        out_specs=VMEM,
        scratch_shapes=[
            pltpu.VMEM((shells, funcs, terms), f32),
            pltpu.VMEM(got.shape, f32),
            pltpu.VMEM((2, count, size), f32),
            pltpu.VMEM((funcs, count, size), f32),
            pltpu.VMEM((count, size), f32),
            pltpu.VMEM((size // 128, count * funcs, 128), f32),
            pltpu.VMEM((count, size), f32),
            pltpu.VMEM((out_rows, size), f32),
        ],
        compiler_params=PARAMS,
        cost_estimate=pl.CostEstimate(
            flops=16 * count * size * size * terms,
            bytes_accessed=2 * shells * funcs * terms,
            transcendentals=count * size * size,
        ),
        name="tasks",
    )(tasks, slots, places, factors, got)


def sum_kernel(index_a, index_b, block_a, block_b, out_ref):
    rows = out_ref.shape[0]
    first = pl.program_id(0) * rows
    total = None
    for index, block in ((index_a, block_a), (index_b, block_b)):
        picked = hot(index[...] == iota((rows, index.shape[1]), 0) + first)
        term = dot(picked, block[...], NN)
        total = term if total is None else total + term
    out_ref[...] = total


def sum_blocks(indices, blocks, total):
    rows = 128
    size = blocks[0].shape[1]
    whole = lambda array: pl.BlockSpec(array.shape, lambda k: (0, 0))
    return pl.pallas_call(
        sum_kernel,
        grid=(total // rows,),
        out_shape=jax.ShapeDtypeStruct((total, size), jnp.float32),
        in_specs=[whole(indices[0]), whole(indices[1]), whole(blocks[0]), whole(blocks[1])],
        out_specs=pl.BlockSpec((rows, size), lambda k: (k, 0)),
        compiler_params=PARAMS,
        name="sum_blocks",
    )(*indices, *blocks)


def trade(array, axis):
    return lax.all_to_all(array, axis, split_axis=0, concat_axis=0, tiled=True)


def body(quartet_tasks, factors, density):
    quartets = quartet_tasks.reshape(-1, 4)
    task_count = quartets.shape[0]
    half = task_count // 2
    bra_count = lax.axis_size("bra")
    ket_count = lax.axis_size("ket")
    rows_per_device, cols_dev, size = (density.shape[0], density.shape[1], density.shape[3])
    table = density.reshape(rows_per_device * cols_dev, size)
    shell_i, shell_j, shell_c, shell_d = (quartets[:, k] for k in range(4))

    cap_bra = 3 * task_count // bra_count
    cap_ket = 5 * task_count // (4 * ket_count)
    half_of = jnp.arange(2 * task_count, dtype=jnp.int32) // task_count
    wanted_shell = jnp.stack([shell_c, shell_j], axis=1).reshape(-1)
    wanted = wanted_shell % rows_per_device * cols_dev + jnp.repeat(shell_d // ket_count, 2)
    bra_bucket = wanted_shell // rows_per_device * 2 + half_of
    target = jnp.stack([shell_j, shell_c], axis=1).reshape(-1)
    position = jnp.repeat(shell_i % rows_per_device, 2) * cols_dev + target // ket_count
    ket_bucket = target % ket_count * 2 + half_of
    slots, asked = plan(
        [bra_bucket[None], ket_bucket[None]],
        [wanted[None], position[None]],
        ((2 * bra_count, cap_bra), (2 * ket_count, cap_ket)),
    )
    asked_bra = trade(asked[0].reshape(bra_count, 2 * cap_bra), "bra")
    asked_bra = asked_bra.reshape(bra_count, 2, cap_bra).transpose(1, 0, 2)
    arrived = trade(asked[1].reshape(ket_count, 2 * cap_ket), "ket")
    arrived = arrived.reshape(ket_count, 2, cap_ket).transpose(1, 0, 2)

    def per_half(slot, capacity, which):
        bucket, place = slot // capacity, slot % capacity
        local = bucket // 2 * capacity + place
        return local[which * task_count : (which + 1) * task_count]

    results = []
    for which in range(2):
        served = serve(asked_bra[which].reshape(1, -1), table)
        got = trade(served.reshape(bra_count, cap_bra, size), "bra")
        outgoing = run_tasks(
            quartets[which * half : (which + 1) * half].reshape(-1),
            per_half(slots[0].reshape(-1), cap_bra, which),
            per_half(slots[1].reshape(-1), cap_ket, which),
            factors,
            got.reshape(-1, size),
            ket_count * cap_ket,
            4,
        )
        back = trade(outgoing.reshape(ket_count, cap_ket, size), "ket")
        results.append(back.reshape(-1, size))
    fock = sum_blocks(
        [arrived[0].reshape(1, -1), arrived[1].reshape(1, -1)],
        results,
        rows_per_device * cols_dev,
    )
    return fock.reshape(rows_per_device, cols_dev, 1, size)


def solution(mesh):
    placed = (P("bra", "ket", None, None), P(), P("bra", None, "ket", None))
    return jax.shard_map(
        body, mesh=mesh, in_specs=placed, out_specs=P("bra", None, "ket", None), check_vma=False
    )
```

```python
import functools

import jax
import jax.numpy as jnp
from jax import lax
from jax.experimental import pallas as pl
from jax.experimental.pallas import tpu as pltpu
from jax.sharding import PartitionSpec as P

tile_scale = 0.0625
NT = (((1,), (1,)), ((), ()))
NN = (((1,), (0,)), ((), ()))
VMEM = pl.BlockSpec(memory_space=pltpu.VMEM)
SMEM = pl.BlockSpec(memory_space=pltpu.SMEM)
PARAMS = pltpu.CompilerParams(vmem_limit_bytes=48 * 1024 * 1024)


def iota(shape, axis):
    return lax.broadcasted_iota(jnp.int32, shape, axis)


def dot(left, right, dims):
    return lax.dot_general(left, right, dims, preferred_element_type=jnp.float32)


def hot(mask):
    return jnp.where(mask, 1.0, 0.0).astype(jnp.bfloat16)


def plan_kernel(sides, bucket_refs, wanted_refs, slot_refs, asked_refs):
    items = bucket_refs[0].shape[1]
    upper = hot(iota((items, items), 0) <= iota((items, items), 1))
    for side, (buckets, capacity) in enumerate(sides):
        owner_id = iota((buckets, items), 0)
        marked = jnp.where(bucket_refs[side][...] == owner_id, 1.0, 0.0)
        counted = dot(marked.astype(jnp.bfloat16), upper, NN)
        offset = (owner_id * capacity - 1).astype(jnp.float32)
        slot = jnp.sum(marked * (counted + offset), axis=0, keepdims=True).astype(jnp.int32)
        slot_refs[side][...] = slot
        wanted = wanted_refs[side][...]
        which = iota((16, items), 0)
        high, low = wanted >> 6, wanted & 63
        values = jnp.where(which == 0, high, jnp.where(which == 1, low, 0))
        values = values.astype(jnp.float32).astype(jnp.bfloat16)
        width = 256

        def part(k, carry, side=side, slot=slot, values=values):
            first = pl.multiple_of(k * width, width)
            picked = hot(slot == iota((width, items), 0) + first)
            found = dot(values, picked, NT)
            asked_refs[side][:, pl.ds(first, width)] = (
                found[0:1] * 64.0 + found[1:2]
            ).astype(jnp.int32)
            return carry

        lax.fori_loop(0, buckets * capacity // width, part, 0)


def plan(buckets, wanted, sides):
    count = len(sides)
    items = buckets[0].shape[1]

    def kernel(*refs):
        plan_kernel(
            sides,
            refs[:count],
            refs[count : 2 * count],
            refs[2 * count : 3 * count],
            refs[3 * count :],
        )

    out = pl.pallas_call(
        kernel,
        out_shape=[jax.ShapeDtypeStruct((1, items), jnp.int32)] * count
        + [jax.ShapeDtypeStruct((1, b * c), jnp.int32) for b, c in sides],
        in_specs=[VMEM] * (2 * count),
        out_specs=[VMEM] * (2 * count),
        compiler_params=PARAMS,
        name="plan",
    )(*buckets, *wanted)
    return out[:count], out[count:]


def serve_kernel(ids_ref, table_ref, out_ref):
    rows = ids_ref.shape[1]
    blocks = table_ref.shape[0]
    spread = jnp.broadcast_to(ids_ref[...], (128, rows)).T
    spread = jnp.concatenate([spread] * (blocks // 128), axis=1)
    picked = hot(spread == iota((rows, blocks), 1))
    out_ref[...] = dot(picked, table_ref[...], NN).astype(jnp.bfloat16)


def serve(ids, table):
    wide = 256
    total = ids.shape[1]
    return pl.pallas_call(
        serve_kernel,
        grid=(total // wide,),
        out_shape=jax.ShapeDtypeStruct((total, table.shape[1]), jnp.bfloat16),
        in_specs=[
            pl.BlockSpec((1, wide), lambda k: (0, k)),
            pl.BlockSpec(table.shape, lambda k: (0, 0)),
        ],
        out_specs=pl.BlockSpec((wide, table.shape[1]), lambda k: (k, 0)),
        compiler_params=PARAMS,
        cost_estimate=pl.CostEstimate(
            flops=2 * total * table.shape[0] * table.shape[1],
            bytes_accessed=4 * total * table.shape[1],
            transcendentals=0,
        ),
        name="serve",
    )(ids, table)


def pair_rows(slow_ref, slow, fast):
    funcs = fast.shape[0]
    parts = []
    for at in range(funcs):
        row = jnp.broadcast_to(slow_ref[slow, at : at + 1, :], fast.shape).astype(jnp.bfloat16)
        parts.append(row * fast)
    return jnp.concatenate(parts, axis=0)


def task_kernel(
    tasks_ref, slots_ref, places_ref, fac_ref, got_ref, out_ref,
    fac32, got32, dens, spread, dens_cd, partial, coulomb, routed,
    raw_a, raw_b, tile_a, tile_b, unroll,
):
    shells, funcs, terms = fac_ref.shape
    size = funcs * funcs
    count = spread.shape[1]
    raws, tiles = (raw_a, raw_b), (tile_a, tile_b)
    fac32[...] = fac_ref[...].astype(jnp.float32)
    got32[...] = got_ref[...].astype(jnp.float32)

    def gather(t, carry):
        for side in range(2):
            dens[side, pl.ds(t, 1), :] = got32[pl.ds(slots_ref[2 * t + side], 1), :]
        return carry

    lax.fori_loop(0, count, gather, 0, unroll=8)
    row, col = iota((size, size), 0), iota((size, size), 1)
    row_hi, row_lo, col_hi, col_lo = row // funcs, row % funcs, col // funcs, col % funcs
    swap = hot((row_hi == col_lo) & (row_lo == col_hi))
    dens_cd[...] = dot(dens[0].astype(jnp.bfloat16), swap, NN)
    dens_jd = dens[1].astype(jnp.bfloat16)

    def spread_one(f, carry):
        spread[f] = dot(dens_jd, hot((row_hi == col_lo) & (row_lo == f)), NN)
        return carry

    lax.fori_loop(0, funcs, spread_one, 0)

    def form(t, raw_ref, k):
        shell_i, shell_j = tasks_ref[4 * t], tasks_ref[4 * t + 1]
        shell_c, shell_d = tasks_ref[4 * t + 2], tasks_ref[4 * t + 3]
        ket = pair_rows(fac32, shell_d, fac_ref[shell_c])
        bra = pair_rows(fac32, shell_i, fac_ref[shell_j])
        raw_ref[k] = dot(ket, bra, NT).astype(raw_ref.dtype)

    def bound(t, raw_ref, tile_ref, k):
        total = None
        for f in range(0, funcs, 2):
            terms_of = []
            for g in (f, f + 1):
                rows = slice(g * funcs, (g + 1) * funcs)
                raw = raw_ref[k, rows, :]
                tile = raw * lax.rsqrt(raw * raw + jnp.ones_like(raw))
                tile_ref[k, rows, :] = tile
                held = jnp.broadcast_to(spread[g, pl.ds(t, 1), :], (funcs, size))
                terms_of.append(tile * held.astype(tile.dtype))
            term = (terms_of[0] + terms_of[1]).astype(jnp.float32)
            total = term if total is None else total + term
        place = pl.ds(pl.multiple_of(t * funcs, funcs), funcs)
        for lane in range(size // 128):
            partial[lane, place, :] = total[:, lane * 128 : (lane + 1) * 128]

    def contract(t, tile_ref, k):
        weights = jnp.broadcast_to(dens_cd[pl.ds(t, 1), :], (16, size)).astype(jnp.bfloat16)
        summed = dot(weights, tile_ref[k], NN)
        coulomb[pl.ds(t, 1), :] = summed[0:1]

    batches = count // unroll

    def first_of(batch):
        return jnp.clip(batch, 0, batches - 1) * unroll

    def steps(pair, carry):
        for odd in range(2):
            batch = 2 * pair + odd
            here, there = (0, 1) if odd == 0 else (1, 0)
            for k in range(unroll):
                contract(first_of(batch - 2) + k, tiles[here], k)
                bound(first_of(batch - 1) + k, raws[there], tiles[there], k)
                form(first_of(batch) + k, raws[here], k)
        return carry

    lax.fori_loop(0, (batches + 2) // 2, steps, 0)

    dens[0] = coulomb[...] * tile_scale
    dens[1] = jnp.zeros((count, size), jnp.float32)

    def fold(e, carry):
        picked = pl.ds(e, count, stride=funcs)
        rows = [partial[lane, picked, :] for lane in range(size // 128)]
        rows = jnp.concatenate(rows, axis=1).astype(jnp.bfloat16)
        dens[1] += dot(rows, hot((row_hi == col_hi) & (col_lo == e)), NN)
        return carry

    lax.fori_loop(0, funcs, fold, 0)
    dens[1] = dens[1] * (-0.5 * tile_scale)
    routed[...] = jnp.zeros_like(routed)

    def route(t, carry):
        for side in range(2):
            routed[pl.ds(places_ref[2 * t + side], 1), :] = dens[side, pl.ds(t, 1), :]
        return carry

    lax.fori_loop(0, count, route, 0, unroll=8)
    out_ref[...] = routed[...].astype(jnp.bfloat16)


def run_tasks(tasks, slots, places, factors, got, out_rows, unroll):
    count = tasks.shape[0] // 4
    shells, funcs, terms = factors.shape
    size = funcs * funcs
    f32 = jnp.float32
    return pl.pallas_call(
        functools.partial(task_kernel, unroll=unroll),
        out_shape=jax.ShapeDtypeStruct((out_rows, size), jnp.bfloat16),
        in_specs=[SMEM, SMEM, SMEM, VMEM, VMEM],
        out_specs=VMEM,
        scratch_shapes=[
            pltpu.VMEM((shells, funcs, terms), f32),
            pltpu.VMEM(got.shape, f32),
            pltpu.VMEM((2, count, size), f32),
            pltpu.VMEM((funcs, count, size), f32),
            pltpu.VMEM((count, size), f32),
            pltpu.VMEM((size // 128, count * funcs, 128), f32),
            pltpu.VMEM((count, size), f32),
            pltpu.VMEM((out_rows, size), f32),
        ]
        + [pltpu.VMEM((unroll, size, size), jnp.bfloat16)] * 4,
        compiler_params=PARAMS,
        cost_estimate=pl.CostEstimate(
            flops=16 * count * size * size * terms,
            bytes_accessed=2 * shells * funcs * terms,
            transcendentals=count * size * size,
        ),
        name="tasks",
    )(tasks, slots, places, factors, got)


def sum_kernel(index_a, index_b, block_a, block_b, out_ref):
    rows = out_ref.shape[0]
    first = pl.program_id(0) * rows
    total = None
    for index, block in ((index_a, block_a), (index_b, block_b)):
        picked = hot(index[...] == iota((rows, index.shape[1]), 0) + first)
        term = dot(picked, block[...], NN)
        total = term if total is None else total + term
    out_ref[...] = total


def sum_blocks(indices, blocks, total):
    rows = 128
    size = blocks[0].shape[1]
    whole = lambda array: pl.BlockSpec(array.shape, lambda k: (0, 0))
    return pl.pallas_call(
        sum_kernel,
        grid=(total // rows,),
        out_shape=jax.ShapeDtypeStruct((total, size), jnp.float32),
        in_specs=[whole(indices[0]), whole(indices[1]), whole(blocks[0]), whole(blocks[1])],
        out_specs=pl.BlockSpec((rows, size), lambda k: (k, 0)),
        compiler_params=PARAMS,
        name="sum_blocks",
    )(*indices, *blocks)


def trade(array, axis):
    return lax.all_to_all(array, axis, split_axis=0, concat_axis=0, tiled=True)


def body(quartet_tasks, factors, density):
    quartets = quartet_tasks.reshape(-1, 4)
    task_count = quartets.shape[0]
    half = task_count // 2
    bra_count = lax.axis_size("bra")
    ket_count = lax.axis_size("ket")
    rows_per_device, cols_dev, size = (density.shape[0], density.shape[1], density.shape[3])
    table = density.reshape(rows_per_device * cols_dev, size)
    shell_i, shell_j, shell_c, shell_d = (quartets[:, k] for k in range(4))

    cap_bra = 3 * task_count // bra_count
    cap_ket = 5 * task_count // (4 * ket_count)
    half_of = jnp.arange(2 * task_count, dtype=jnp.int32) // task_count
    wanted_shell = jnp.stack([shell_c, shell_j], axis=1).reshape(-1)
    wanted = wanted_shell % rows_per_device * cols_dev + jnp.repeat(shell_d // ket_count, 2)
    bra_bucket = wanted_shell // rows_per_device * 2 + half_of
    target = jnp.stack([shell_j, shell_c], axis=1).reshape(-1)
    position = jnp.repeat(shell_i % rows_per_device, 2) * cols_dev + target // ket_count
    ket_bucket = target % ket_count * 2 + half_of
    slot_bra, asked_bra = plan(
        [bra_bucket[None]], [wanted[None]], ((2 * bra_count, cap_bra),)
    )
    asked_bra = trade(asked_bra[0].reshape(bra_count, 2 * cap_bra), "bra")
    asked_bra = asked_bra.reshape(bra_count, 2, cap_bra).transpose(1, 0, 2)
    served = [serve(asked_bra[which].reshape(1, -1), table) for which in range(2)]
    late_bucket, served[0] = lax.optimization_barrier((ket_bucket, served[0]))
    slot_ket, asked_ket = plan(
        [late_bucket[None]], [position[None]], ((2 * ket_count, cap_ket),)
    )
    slots = (slot_bra[0], slot_ket[0])

    def per_half(slot, capacity, which):
        bucket, place = slot // capacity, slot % capacity
        local = bucket // 2 * capacity + place
        return local[which * task_count : (which + 1) * task_count]

    results = []
    for which in range(2):
        got = trade(served[which].reshape(bra_count, cap_bra, size), "bra")
        outgoing = run_tasks(
            quartets[which * half : (which + 1) * half].reshape(-1),
            per_half(slots[0].reshape(-1), cap_bra, which),
            per_half(slots[1].reshape(-1), cap_ket, which),
            factors,
            got.reshape(-1, size),
            ket_count * cap_ket,
            4,
        )
        if which == 0:
            sent, outgoing = lax.optimization_barrier((asked_ket[0], outgoing))
            arrived = trade(sent.reshape(ket_count, 2 * cap_ket), "ket")
            arrived = arrived.reshape(ket_count, 2, cap_ket).transpose(1, 0, 2)
        back = trade(outgoing.reshape(ket_count, cap_ket, size), "ket")
        results.append(back.reshape(-1, size))
    fock = sum_blocks(
        [arrived[0].reshape(1, -1), arrived[1].reshape(1, -1)],
        results,
        rows_per_device * cols_dev,
    )
    return fock.reshape(rows_per_device, cols_dev, 1, size)


def solution(mesh):
    placed = (P("bra", "ket", None, None), P(), P("bra", None, "ket", None))
    return jax.shard_map(
        body, mesh=mesh, in_specs=placed, out_specs=P("bra", None, "ket", None), check_vma=False
    )
```

```python
import functools

import jax
import jax.numpy as jnp
from jax import lax
from jax.experimental import pallas as pl
from jax.experimental.pallas import tpu as pltpu
from jax.sharding import PartitionSpec as P

tile_scale = 0.0625
NT = (((1,), (1,)), ((), ()))
NN = (((1,), (0,)), ((), ()))
id_rows = 16
VMEM = pl.BlockSpec(memory_space=pltpu.VMEM)
SMEM = pl.BlockSpec(memory_space=pltpu.SMEM)
PARAMS = pltpu.CompilerParams(vmem_limit_bytes=48 * 1024 * 1024)


def iota(shape, axis):
    return lax.broadcasted_iota(jnp.int32, shape, axis)


def dot(left, right, dims):
    return lax.dot_general(left, right, dims, preferred_element_type=jnp.float32)


def hot(mask):
    return jnp.where(mask, 1.0, 0.0).astype(jnp.bfloat16)


def plan_kernel(sides, bucket_refs, wanted_refs, slot_refs, asked_refs):
    items = bucket_refs[0].shape[1]
    upper = hot(iota((items, items), 0) <= iota((items, items), 1))
    for side, (buckets, capacity) in enumerate(sides):
        owner_id = iota((buckets, items), 0)
        marked = jnp.where(bucket_refs[side][...] == owner_id, 1.0, 0.0)
        counted = dot(marked.astype(jnp.bfloat16), upper, NN)
        offset = (owner_id * capacity - 1).astype(jnp.float32)
        slot = jnp.sum(marked * (counted + offset), axis=0, keepdims=True).astype(jnp.int32)
        slot_refs[side][...] = slot
        wanted = wanted_refs[side][...]
        which = iota((16, items), 0)
        high, low = wanted >> 6, wanted & 63
        values = jnp.where(which == 0, high, jnp.where(which == 1, low, 0))
        values = values.astype(jnp.float32).astype(jnp.bfloat16)
        width = 256

        def part(k, carry, side=side, slot=slot, values=values):
            first = pl.multiple_of(k * width, width)
            picked = hot(slot == iota((width, items), 0) + first)
            found = dot(values, picked, NT)
            asked_refs[side][:, pl.ds(first, width)] = (
                found[0:1] * 64.0 + found[1:2]
            ).astype(jnp.int32)
            return carry

        lax.fori_loop(0, buckets * capacity // width, part, 0)


def plan(buckets, wanted, sides):
    count = len(sides)
    items = buckets[0].shape[1]

    def kernel(*refs):
        plan_kernel(
            sides,
            refs[:count],
            refs[count : 2 * count],
            refs[2 * count : 3 * count],
            refs[3 * count :],
        )

    out = pl.pallas_call(
        kernel,
        out_shape=[jax.ShapeDtypeStruct((1, items), jnp.int32)] * count
        + [jax.ShapeDtypeStruct((1, b * c), jnp.int32) for b, c in sides],
        in_specs=[VMEM] * (2 * count),
        out_specs=[VMEM] * (2 * count),
        compiler_params=PARAMS,
        name="plan",
    )(*buckets, *wanted)
    return out[:count], out[count:]


def serve_kernel(ids_ref, table_ref, out_ref):
    rows = ids_ref.shape[1]
    blocks = table_ref.shape[0]
    spread = jnp.broadcast_to(ids_ref[...], (128, rows)).T
    spread = jnp.concatenate([spread] * (blocks // 128), axis=1)
    picked = hot(spread == iota((rows, blocks), 1))
    out_ref[...] = dot(picked, table_ref[...], NN).astype(jnp.bfloat16)


def serve(ids, table):
    wide = 256
    total = ids.shape[1]
    return pl.pallas_call(
        serve_kernel,
        grid=(total // wide,),
        out_shape=jax.ShapeDtypeStruct((total, table.shape[1]), jnp.bfloat16),
        in_specs=[
            pl.BlockSpec((1, wide), lambda k: (0, k)),
            pl.BlockSpec(table.shape, lambda k: (0, 0)),
        ],
        out_specs=pl.BlockSpec((wide, table.shape[1]), lambda k: (k, 0)),
        compiler_params=PARAMS,
        cost_estimate=pl.CostEstimate(
            flops=2 * total * table.shape[0] * table.shape[1],
            bytes_accessed=4 * total * table.shape[1],
            transcendentals=0,
        ),
        name="serve",
    )(ids, table)


def pair_rows(slow_ref, slow, fast):
    funcs = fast.shape[0]
    parts = []
    for at in range(funcs):
        row = jnp.broadcast_to(slow_ref[slow, at : at + 1, :], fast.shape).astype(jnp.bfloat16)
        parts.append(row * fast)
    return jnp.concatenate(parts, axis=0)


def task_kernel(
    tasks_ref, slots_ref, places_ref, fac_ref, got_ref, ids_ref, out_ref,
    fac32, got32, dens, spread, dens_cd, partial, coulomb, routed,
    raw_a, raw_b, tile_a, tile_b, unroll,
):
    shells, funcs, terms = fac_ref.shape
    size = funcs * funcs
    count = spread.shape[1]
    raws, tiles = (raw_a, raw_b), (tile_a, tile_b)
    fac32[...] = fac_ref[...].astype(jnp.float32)
    got32[...] = got_ref[...].astype(jnp.float32)

    def gather(t, carry):
        for side in range(2):
            dens[side, pl.ds(t, 1), :] = got32[pl.ds(slots_ref[2 * t + side], 1), :]
        return carry

    lax.fori_loop(0, count, gather, 0, unroll=8)
    row, col = iota((size, size), 0), iota((size, size), 1)
    row_hi, row_lo, col_hi, col_lo = row // funcs, row % funcs, col // funcs, col % funcs
    swap = hot((row_hi == col_lo) & (row_lo == col_hi))
    dens_cd[...] = dot(dens[0].astype(jnp.bfloat16), swap, NN)
    dens_jd = dens[1].astype(jnp.bfloat16)

    def spread_one(f, carry):
        spread[f] = dot(dens_jd, hot((row_hi == col_lo) & (row_lo == f)), NN)
        return carry

    lax.fori_loop(0, funcs, spread_one, 0, unroll=4)

    def form(t, raw_ref, k):
        shell_i, shell_j = tasks_ref[4 * t], tasks_ref[4 * t + 1]
        shell_c, shell_d = tasks_ref[4 * t + 2], tasks_ref[4 * t + 3]
        ket = pair_rows(fac32, shell_d, fac_ref[shell_c])
        bra = pair_rows(fac32, shell_i, fac_ref[shell_j])
        raw_ref[k] = dot(ket, bra, NT).astype(raw_ref.dtype)

    def bound(t, raw_ref, tile_ref, k):
        total = None
        for f in range(0, funcs, 2):
            terms_of = []
            for g in (f, f + 1):
                rows = slice(g * funcs, (g + 1) * funcs)
                raw = raw_ref[k, rows, :]
                tile = raw * lax.rsqrt(raw * raw + jnp.ones_like(raw))
                tile_ref[k, rows, :] = tile
                held = jnp.broadcast_to(spread[g, pl.ds(t, 1), :], (funcs, size))
                terms_of.append(tile * held.astype(tile.dtype))
            term = (terms_of[0] + terms_of[1]).astype(jnp.float32)
            total = term if total is None else total + term
        place = pl.ds(pl.multiple_of(t * funcs, funcs), funcs)
        for lane in range(size // 128):
            partial[lane, place, :] = total[:, lane * 128 : (lane + 1) * 128]

    def contract(t, tile_ref, k):
        weights = jnp.broadcast_to(dens_cd[pl.ds(t, 1), :], (16, size)).astype(jnp.bfloat16)
        summed = dot(weights, tile_ref[k], NN)
        coulomb[pl.ds(t, 1), :] = summed[0:1]

    batches = count // unroll

    def first_of(batch):
        return jnp.clip(batch, 0, batches - 1) * unroll

    def steps(pair, carry):
        for odd in range(2):
            batch = 2 * pair + odd
            here, there = (0, 1) if odd == 0 else (1, 0)
            for k in range(unroll):
                contract(first_of(batch - 2) + k, tiles[here], k)
                bound(first_of(batch - 1) + k, raws[there], tiles[there], k)
                form(first_of(batch) + k, raws[here], k)
        return carry

    lax.fori_loop(0, (batches + 2) // 2, steps, 0)

    dens[0] = coulomb[...] * tile_scale
    dens[1] = jnp.zeros((count, size), jnp.float32)

    def fold(e, carry):
        picked = pl.ds(e, count, stride=funcs)
        rows = [partial[lane, picked, :] for lane in range(size // 128)]
        rows = jnp.concatenate(rows, axis=1).astype(jnp.bfloat16)
        dens[1] += dot(rows, hot((row_hi == col_hi) & (col_lo == e)), NN)
        return carry

    lax.fori_loop(0, funcs, fold, 0, unroll=4)
    dens[1] = dens[1] * (-0.5 * tile_scale)
    routed[...] = jnp.zeros_like(routed)
    owners = ids_ref.shape[0] // 2
    stride = routed.shape[0] // owners
    for owner in range(owners):
        last = (owner + 1) * stride - id_rows
        routed[last : last + 2, :] = ids_ref[2 * owner : 2 * owner + 2, :]

    def route(t, carry):
        for side in range(2):
            routed[pl.ds(places_ref[2 * t + side], 1), :] = dens[side, pl.ds(t, 1), :]
        return carry

    lax.fori_loop(0, count, route, 0, unroll=8)
    out_ref[...] = routed[...].astype(jnp.bfloat16)


def run_tasks(tasks, slots, places, factors, got, ids, out_rows, unroll):
    count = tasks.shape[0] // 4
    shells, funcs, terms = factors.shape
    size = funcs * funcs
    f32 = jnp.float32
    return pl.pallas_call(
        functools.partial(task_kernel, unroll=unroll),
        out_shape=jax.ShapeDtypeStruct((out_rows, size), jnp.bfloat16),
        in_specs=[SMEM, SMEM, SMEM, VMEM, VMEM, VMEM],
        out_specs=VMEM,
        scratch_shapes=[
            pltpu.VMEM((shells, funcs, terms), f32),
            pltpu.VMEM(got.shape, f32),
            pltpu.VMEM((2, count, size), f32),
            pltpu.VMEM((funcs, count, size), f32),
            pltpu.VMEM((count, size), f32),
            pltpu.VMEM((size // 128, count * funcs, 128), f32),
            pltpu.VMEM((count, size), f32),
            pltpu.VMEM((out_rows, size), f32),
        ]
        + [pltpu.VMEM((unroll, size, size), jnp.bfloat16)] * 4,
        compiler_params=PARAMS,
        cost_estimate=pl.CostEstimate(
            flops=16 * count * size * size * terms,
            bytes_accessed=2 * shells * funcs * terms,
            transcendentals=count * size * size,
        ),
        name="tasks",
    )(tasks, slots, places, factors, got, ids)


def sum_kernel(block_a, block_b, out_ref, *, sources):
    rows = out_ref.shape[0]
    stride = block_a.shape[0] // sources
    first = pl.program_id(0) * rows
    here = (iota((rows, stride), 0) + first).astype(jnp.float32)
    total = None
    for block in (block_a, block_b):
        for source in range(sources):
            held = block[source * stride : (source + 1) * stride, :]
            ids = held[stride - id_rows :, :].astype(jnp.float32)
            index = (ids[0:1] * 64.0 + ids[1:2])[:, :stride]
            term = dot(hot(jnp.broadcast_to(index, here.shape) == here), held, NN)
            total = term if total is None else total + term
    out_ref[...] = total


def sum_blocks(blocks, sources, total):
    rows = 128
    size = blocks[0].shape[1]
    whole = lambda array: pl.BlockSpec(array.shape, lambda k: (0, 0))
    return pl.pallas_call(
        functools.partial(sum_kernel, sources=sources),
        grid=(total // rows,),
        out_shape=jax.ShapeDtypeStruct((total, size), jnp.float32),
        in_specs=[whole(blocks[0]), whole(blocks[1])],
        out_specs=pl.BlockSpec((rows, size), lambda k: (k, 0)),
        compiler_params=PARAMS,
        name="sum_blocks",
    )(*blocks)


def trade(array, axis):
    return lax.all_to_all(array, axis, split_axis=0, concat_axis=0, tiled=True)


def body(quartet_tasks, factors, density):
    quartets = quartet_tasks.reshape(-1, 4)
    task_count = quartets.shape[0]
    half = task_count // 2
    bra_count = lax.axis_size("bra")
    ket_count = lax.axis_size("ket")
    rows_per_device, cols_dev, size = (density.shape[0], density.shape[1], density.shape[3])
    table = density.reshape(rows_per_device * cols_dev, size)
    shell_i, shell_j, shell_c, shell_d = (quartets[:, k] for k in range(4))

    cap_bra = 3 * task_count // bra_count
    cap_ket = 5 * task_count // (4 * ket_count)
    half_of = jnp.arange(2 * task_count, dtype=jnp.int32) // task_count
    wanted_shell = jnp.stack([shell_c, shell_j], axis=1).reshape(-1)
    wanted = wanted_shell % rows_per_device * cols_dev + jnp.repeat(shell_d // ket_count, 2)
    bra_bucket = wanted_shell // rows_per_device * 2 + half_of
    target = jnp.stack([shell_j, shell_c], axis=1).reshape(-1)
    position = jnp.repeat(shell_i % rows_per_device, 2) * cols_dev + target // ket_count
    ket_bucket = target % ket_count * 2 + half_of
    slot_bra, asked_bra = plan(
        [bra_bucket[None]], [wanted[None]], ((2 * bra_count, cap_bra),)
    )
    asked_bra = trade(asked_bra[0].reshape(bra_count, 2 * cap_bra), "bra")
    asked_bra = asked_bra.reshape(bra_count, 2, cap_bra).transpose(1, 0, 2)
    served = [serve(asked_bra[which].reshape(1, -1), table) for which in range(2)]
    late_bucket, served[0] = lax.optimization_barrier((ket_bucket, served[0]))
    slot_ket, asked_ket = plan(
        [late_bucket[None]], [position[None]], ((2 * ket_count, cap_ket),)
    )
    slots = (slot_bra[0], slot_ket[0])

    def per_half(slot, capacity, stride, which):
        bucket, place = slot // capacity, slot % capacity
        local = bucket // 2 * stride + place
        return local[which * task_count : (which + 1) * task_count]

    stride = cap_ket + id_rows
    ids = asked_ket[0].reshape(ket_count, 2, cap_ket)
    ids = jnp.stack([ids >> 6, ids & 63], axis=2).astype(jnp.float32)
    ids = jnp.pad(ids, ((0, 0), (0, 0), (0, 0), (0, size - cap_ket)), constant_values=-1.0)

    results = []
    for which in range(2):
        got = trade(served[which].reshape(bra_count, cap_bra, size), "bra")
        outgoing = run_tasks(
            quartets[which * half : (which + 1) * half].reshape(-1),
            per_half(slots[0].reshape(-1), cap_bra, cap_bra, which),
            per_half(slots[1].reshape(-1), cap_ket, stride, which),
            factors,
            got.reshape(-1, size),
            ids[:, which].reshape(-1, size),
            ket_count * stride,
            4,
        )
        back = trade(outgoing.reshape(ket_count, stride, size), "ket")
        results.append(back.reshape(-1, size))
    fock = sum_blocks(results, ket_count, rows_per_device * cols_dev)
    return fock.reshape(rows_per_device, cols_dev, 1, size)


def solution(mesh):
    placed = (P("bra", "ket", None, None), P(), P("bra", None, "ket", None))
    return jax.shard_map(
        body, mesh=mesh, in_specs=placed, out_specs=P("bra", None, "ket", None), check_vma=False
    )
```

```python
import functools

import jax
import jax.numpy as jnp
from jax import lax
from jax.experimental import pallas as pl
from jax.experimental.pallas import tpu as pltpu
from jax.sharding import PartitionSpec as P

tile_scale = 0.0625
NT = (((1,), (1,)), ((), ()))
NN = (((1,), (0,)), ((), ()))
id_rows = 16
VMEM = pl.BlockSpec(memory_space=pltpu.VMEM)
SMEM = pl.BlockSpec(memory_space=pltpu.SMEM)
PARAMS = pltpu.CompilerParams(vmem_limit_bytes=48 * 1024 * 1024)


def iota(shape, axis):
    return lax.broadcasted_iota(jnp.int32, shape, axis)


def dot(left, right, dims):
    return lax.dot_general(left, right, dims, preferred_element_type=jnp.float32)


def hot(mask):
    return jnp.where(mask, 1.0, 0.0).astype(jnp.bfloat16)


def slots_of(bucket, upper, buckets, capacity):
    owner_id = iota((buckets, bucket.shape[1]), 0)
    marked = jnp.where(bucket == owner_id, 1.0, 0.0)
    counted = dot(marked.astype(jnp.bfloat16), upper, NN)
    offset = (owner_id * capacity - 1).astype(jnp.float32)
    return jnp.sum(marked * (counted + offset), axis=0, keepdims=True).astype(jnp.int32)


def split_values(wanted):
    which = iota((16, wanted.shape[1]), 0)
    values = jnp.where(which == 0, wanted >> 6, jnp.where(which == 1, wanted & 63, 0))
    return values.astype(jnp.float32).astype(jnp.bfloat16)


def listed(slot, values, first, width):
    picked = hot(slot == iota((width, slot.shape[1]), 0) + first)
    found = dot(values, picked, NT)
    return (found[0:1] * 64.0 + found[1:2]).astype(jnp.int32)


def front_kernel(
    bra_bucket, bra_wanted, ket_bucket, ket_wanted, table_ref,
    bra_slot, ket_slot, ket_asked, got_out, later_out,
    asked, heard, answer, got, ask_send, ask_recv, ans_send, ans_recv,
    *, peers, cap_bra, kets, cap_ket,
):
    me = lax.axis_index("bra")
    barrier = pltpu.get_barrier_semaphore()
    for k in range(1, peers):
        pl.semaphore_signal(
            barrier, inc=1, device_id={"bra": lax.rem(me + k, peers)},
            device_id_type=pl.DeviceIdType.MESH,
        )
    items = bra_bucket.shape[1]
    width = asked.shape[2]
    blocks = table_ref.shape[0]
    upper = hot(iota((items, items), 0) <= iota((items, items), 1))
    slot = slots_of(bra_bucket[...], upper, 2 * peers, cap_bra)
    slot_k = slots_of(ket_bucket[...], upper, 2 * kets, cap_ket)
    bra_slot[...] = slot
    ket_slot[...] = slot_k
    values = split_values(bra_wanted[...])

    def ask_list(p, carry):
        ids = listed(slot, values, p * (2 * cap_bra), width)
        asked[p] = jnp.broadcast_to(ids, asked.shape[1:])
        return carry

    lax.fori_loop(0, peers, ask_list, 0)

    def ask(k):
        peer = lax.rem(me + k, peers)
        return pltpu.make_async_remote_copy(
            src_ref=asked.at[peer], dst_ref=heard.at[me],
            send_sem=ask_send.at[k], recv_sem=ask_recv.at[k],
            device_id={"bra": peer}, device_id_type=pl.DeviceIdType.MESH,
        )

    def give(k):
        peer = lax.rem(me + peers - k, peers)
        return pltpu.make_async_remote_copy(
            src_ref=answer.at[peer], dst_ref=got.at[me],
            send_sem=ans_send.at[k], recv_sem=ans_recv.at[k],
            device_id={"bra": peer}, device_id_type=pl.DeviceIdType.MESH,
        )

    def serve(ids, which):
        spread = jnp.broadcast_to(ids[0:1], (128, width)).T
        spread = spread[which * cap_bra : (which + 1) * cap_bra]
        spread = jnp.concatenate([spread] * (blocks // 128), axis=1)
        picked = hot(spread == iota((cap_bra, blocks), 1))
        return dot(picked, table_ref[...], NN).astype(jnp.bfloat16)

    pl.semaphore_wait(barrier, peers - 1)

    def send_ask(k, carry):
        ask(k).start()
        return carry

    lax.fori_loop(1, peers, send_ask, 0)
    got[me] = serve(asked[me], 0)
    later_out[me] = serve(asked[me], 1)

    def reply(k, carry):
        ask(k).wait_recv()
        peer = lax.rem(me + peers - k, peers)
        answer[peer] = serve(heard[peer], 0)
        give(k).start()
        return carry

    lax.fori_loop(1, peers, reply, 0)

    def reply_later(k, carry):
        peer = lax.rem(me + peers - k, peers)
        later_out[peer] = serve(heard[peer], 1)
        return carry

    lax.fori_loop(1, peers, reply_later, 0)
    values_k = split_values(ket_wanted[...])
    part = 256

    def place_list(k, carry):
        first = pl.multiple_of(k * part, part)
        ket_asked[:, pl.ds(first, part)] = listed(slot_k, values_k, first, part)
        return carry

    lax.fori_loop(0, ket_asked.shape[1] // part, place_list, 0)

    def finish(k, carry):
        ask(k).wait_send()
        give(k).wait_send()
        give(k).wait_recv()
        return carry

    lax.fori_loop(1, peers, finish, 0)
    got_out[...] = got[...]


def front(bra_bucket, bra_wanted, ket_bucket, ket_wanted, table, peers, cap_bra, kets, cap_ket):
    items = bra_bucket.shape[1]
    width = -(-2 * cap_bra // 128) * 128
    size = table.shape[1]
    blocks = (peers, cap_bra, size)
    return pl.pallas_call(
        functools.partial(
            front_kernel, peers=peers, cap_bra=cap_bra, kets=kets, cap_ket=cap_ket
        ),
        out_shape=[
            jax.ShapeDtypeStruct((1, items), jnp.int32),
            jax.ShapeDtypeStruct((1, items), jnp.int32),
            jax.ShapeDtypeStruct((1, 2 * kets * cap_ket), jnp.int32),
            jax.ShapeDtypeStruct(blocks, jnp.bfloat16),
            jax.ShapeDtypeStruct(blocks, jnp.bfloat16),
        ],
        in_specs=[VMEM] * 5,
        out_specs=[VMEM] * 5,
        scratch_shapes=[
            pltpu.VMEM((peers, 8, width), jnp.int32),
            pltpu.VMEM((peers, 8, width), jnp.int32),
            pltpu.VMEM(blocks, jnp.bfloat16),
            pltpu.VMEM(blocks, jnp.bfloat16),
        ]
        + [pltpu.SemaphoreType.DMA((peers,))] * 4,
        compiler_params=pltpu.CompilerParams(
            vmem_limit_bytes=48 * 1024 * 1024, collective_id=0, has_side_effects=True
        ),
        name="front",
    )(bra_bucket, bra_wanted, ket_bucket, ket_wanted, table)


def pair_rows(slow_ref, slow, fast):
    funcs = fast.shape[0]
    parts = []
    for at in range(funcs):
        row = jnp.broadcast_to(slow_ref[slow, at : at + 1, :], fast.shape).astype(jnp.bfloat16)
        parts.append(row * fast)
    return jnp.concatenate(parts, axis=0)


def task_kernel(
    tasks_ref, slots_ref, places_ref, fac_ref, got_ref, ids_ref, out_ref,
    fac32, got32, dens, spread, dens_cd, partial, coulomb, routed,
    raw_a, raw_b, tile_a, tile_b, unroll,
):
    shells, funcs, terms = fac_ref.shape
    size = funcs * funcs
    count = spread.shape[1]
    raws, tiles = (raw_a, raw_b), (tile_a, tile_b)
    fac32[...] = fac_ref[...].astype(jnp.float32)
    got32[...] = got_ref[...].astype(jnp.float32)

    def gather(t, carry):
        for side in range(2):
            dens[side, pl.ds(t, 1), :] = got32[pl.ds(slots_ref[2 * t + side], 1), :]
        return carry

    lax.fori_loop(0, count, gather, 0, unroll=8)
    row, col = iota((size, size), 0), iota((size, size), 1)
    row_hi, row_lo, col_hi, col_lo = row // funcs, row % funcs, col // funcs, col % funcs
    swap = hot((row_hi == col_lo) & (row_lo == col_hi))
    dens_cd[...] = dot(dens[0].astype(jnp.bfloat16), swap, NN)
    dens_jd = dens[1].astype(jnp.bfloat16)

    def spread_one(f, carry):
        spread[f] = dot(dens_jd, hot((row_hi == col_lo) & (row_lo == f)), NN)
        return carry

    lax.fori_loop(0, funcs, spread_one, 0, unroll=8)

    def form(t, raw_ref, k):
        shell_i, shell_j = tasks_ref[4 * t], tasks_ref[4 * t + 1]
        shell_c, shell_d = tasks_ref[4 * t + 2], tasks_ref[4 * t + 3]
        ket = pair_rows(fac32, shell_d, fac_ref[shell_c])
        bra = pair_rows(fac32, shell_i, fac_ref[shell_j])
        raw_ref[k] = dot(ket, bra, NT).astype(raw_ref.dtype)

    def bound(t, raw_ref, tile_ref, k):
        total = None
        for f in range(0, funcs, 2):
            terms_of = []
            for g in (f, f + 1):
                rows = slice(g * funcs, (g + 1) * funcs)
                raw = raw_ref[k, rows, :]
                tile = raw * lax.rsqrt(raw * raw + jnp.ones_like(raw))
                tile_ref[k, rows, :] = tile
                held = jnp.broadcast_to(spread[g, pl.ds(t, 1), :], (funcs, size))
                terms_of.append(tile * held.astype(tile.dtype))
            term = (terms_of[0] + terms_of[1]).astype(jnp.float32)
            total = term if total is None else total + term
        place = pl.ds(pl.multiple_of(t * funcs, funcs), funcs)
        for lane in range(size // 128):
            partial[lane, place, :] = total[:, lane * 128 : (lane + 1) * 128]

    def contract(t, tile_ref, k):
        weights = jnp.broadcast_to(dens_cd[pl.ds(t, 1), :], (16, size)).astype(jnp.bfloat16)
        summed = dot(weights, tile_ref[k], NN)
        coulomb[pl.ds(t, 1), :] = summed[0:1]

    batches = count // unroll

    def first_of(batch):
        return jnp.clip(batch, 0, batches - 1) * unroll

    def steps(pair, carry):
        for odd in range(2):
            batch = 2 * pair + odd
            here, there = (0, 1) if odd == 0 else (1, 0)
            for k in range(unroll):
                contract(first_of(batch - 2) + k, tiles[here], k)
                bound(first_of(batch - 1) + k, raws[there], tiles[there], k)
                form(first_of(batch) + k, raws[here], k)
        return carry

    lax.fori_loop(0, (batches + 2) // 2, steps, 0)

    dens[0] = coulomb[...] * tile_scale
    dens[1] = jnp.zeros((count, size), jnp.float32)

    def fold(e, carry):
        picked = pl.ds(e, count, stride=funcs)
        rows = [partial[lane, picked, :] for lane in range(size // 128)]
        rows = jnp.concatenate(rows, axis=1).astype(jnp.bfloat16)
        dens[1] += dot(rows, hot((row_hi == col_hi) & (col_lo == e)), NN)
        return carry

    lax.fori_loop(0, funcs, fold, 0, unroll=8)
    dens[1] = dens[1] * (-0.5 * tile_scale)
    routed[...] = jnp.zeros_like(routed)
    owners = ids_ref.shape[0] // 2
    stride = routed.shape[0] // owners
    for owner in range(owners):
        last = (owner + 1) * stride - id_rows
        routed[last : last + 2, :] = ids_ref[2 * owner : 2 * owner + 2, :]

    def route(t, carry):
        for side in range(2):
            routed[pl.ds(places_ref[2 * t + side], 1), :] = dens[side, pl.ds(t, 1), :]
        return carry

    lax.fori_loop(0, count, route, 0, unroll=8)
    out_ref[...] = routed[...].astype(jnp.bfloat16)


def run_tasks(tasks, slots, places, factors, got, ids, out_rows, unroll):
    count = tasks.shape[0] // 4
    shells, funcs, terms = factors.shape
    size = funcs * funcs
    f32 = jnp.float32
    return pl.pallas_call(
        functools.partial(task_kernel, unroll=unroll),
        out_shape=jax.ShapeDtypeStruct((out_rows, size), jnp.bfloat16),
        in_specs=[SMEM, SMEM, SMEM, VMEM, VMEM, VMEM],
        out_specs=VMEM,
        scratch_shapes=[
            pltpu.VMEM((shells, funcs, terms), f32),
            pltpu.VMEM(got.shape, f32),
            pltpu.VMEM((2, count, size), f32),
            pltpu.VMEM((funcs, count, size), f32),
            pltpu.VMEM((count, size), f32),
            pltpu.VMEM((size // 128, count * funcs, 128), f32),
            pltpu.VMEM((count, size), f32),
            pltpu.VMEM((out_rows, size), f32),
        ]
        + [pltpu.VMEM((unroll, size, size), jnp.bfloat16)] * 4,
        compiler_params=PARAMS,
        cost_estimate=pl.CostEstimate(
            flops=16 * count * size * size * terms,
            bytes_accessed=2 * shells * funcs * terms,
            transcendentals=count * size * size,
        ),
        name="tasks",
    )(tasks, slots, places, factors, got, ids)


def sum_kernel(block_a, block_b, out_ref, *, sources):
    rows = out_ref.shape[0]
    stride = block_a.shape[0] // sources
    first = pl.program_id(0) * rows
    here = (iota((rows, stride), 0) + first).astype(jnp.float32)
    total = None
    for block in (block_a, block_b):
        for source in range(sources):
            held = block[source * stride : (source + 1) * stride, :]
            ids = held[stride - id_rows :, :].astype(jnp.float32)
            index = (ids[0:1] * 64.0 + ids[1:2])[:, :stride]
            term = dot(hot(jnp.broadcast_to(index, here.shape) == here), held, NN)
            total = term if total is None else total + term
    out_ref[...] = total


def sum_blocks(blocks, sources, total):
    rows = 128
    size = blocks[0].shape[1]
    whole = lambda array: pl.BlockSpec(array.shape, lambda k: (0, 0))
    return pl.pallas_call(
        functools.partial(sum_kernel, sources=sources),
        grid=(total // rows,),
        out_shape=jax.ShapeDtypeStruct((total, size), jnp.float32),
        in_specs=[whole(blocks[0]), whole(blocks[1])],
        out_specs=pl.BlockSpec((rows, size), lambda k: (k, 0)),
        compiler_params=PARAMS,
        name="sum_blocks",
    )(*blocks)


def trade(array, axis):
    return lax.all_to_all(array, axis, split_axis=0, concat_axis=0, tiled=True)


def body(quartet_tasks, factors, density):
    quartets = quartet_tasks.reshape(-1, 4)
    task_count = quartets.shape[0]
    half = task_count // 2
    bra_count = lax.axis_size("bra")
    ket_count = lax.axis_size("ket")
    rows_per_device, cols_dev, size = (density.shape[0], density.shape[1], density.shape[3])
    table = density.reshape(rows_per_device * cols_dev, size)
    shell_i, shell_j, shell_c, shell_d = (quartets[:, k] for k in range(4))

    cap_bra = 3 * task_count // bra_count
    cap_ket = 5 * task_count // (4 * ket_count)
    half_of = jnp.arange(2 * task_count, dtype=jnp.int32) // task_count
    wanted_shell = jnp.stack([shell_c, shell_j], axis=1).reshape(-1)
    wanted = wanted_shell % rows_per_device * cols_dev + jnp.repeat(shell_d // ket_count, 2)
    bra_bucket = wanted_shell // rows_per_device * 2 + half_of
    target = jnp.stack([shell_j, shell_c], axis=1).reshape(-1)
    position = jnp.repeat(shell_i % rows_per_device, 2) * cols_dev + target // ket_count
    ket_bucket = target % ket_count * 2 + half_of
    slot_bra, slot_ket, asked_ket, first_got, later = front(
        bra_bucket[None], wanted[None], ket_bucket[None], position[None], table,
        bra_count, cap_bra, ket_count, cap_ket,
    )
    slots = (slot_bra, slot_ket)

    def per_half(slot, capacity, stride, which):
        bucket, place = slot // capacity, slot % capacity
        local = bucket // 2 * stride + place
        return local[which * task_count : (which + 1) * task_count]

    stride = cap_ket + id_rows
    ids = asked_ket.reshape(ket_count, 2, cap_ket)
    ids = jnp.stack([ids >> 6, ids & 63], axis=2).astype(jnp.float32)
    ids = jnp.pad(ids, ((0, 0), (0, 0), (0, 0), (0, size - cap_ket)), constant_values=-1.0)

    results = []
    for which in range(2):
        got = first_got if which == 0 else trade(later, "bra")
        outgoing = run_tasks(
            quartets[which * half : (which + 1) * half].reshape(-1),
            per_half(slots[0].reshape(-1), cap_bra, cap_bra, which),
            per_half(slots[1].reshape(-1), cap_ket, stride, which),
            factors,
            got.reshape(-1, size),
            ids[:, which].reshape(-1, size),
            ket_count * stride,
            4,
        )
        back = trade(outgoing.reshape(ket_count, stride, size), "ket")
        results.append(back.reshape(-1, size))
    fock = sum_blocks(results, ket_count, rows_per_device * cols_dev)
    return fock.reshape(rows_per_device, cols_dev, 1, size)


def solution(mesh):
    placed = (P("bra", "ket", None, None), P(), P("bra", None, "ket", None))
    return jax.shard_map(
        body, mesh=mesh, in_specs=placed, out_specs=P("bra", None, "ket", None), check_vma=False
    )
```

```python
import functools

import jax
import jax.numpy as jnp
from jax import lax
from jax.experimental import pallas as pl
from jax.experimental.pallas import tpu as pltpu
from jax.sharding import PartitionSpec as P

tile_scale = 0.0625
NT = (((1,), (1,)), ((), ()))
NN = (((1,), (0,)), ((), ()))
id_rows = 16
VMEM = pl.BlockSpec(memory_space=pltpu.VMEM)
SMEM = pl.BlockSpec(memory_space=pltpu.SMEM)
PARAMS = pltpu.CompilerParams(vmem_limit_bytes=48 * 1024 * 1024)


def iota(shape, axis):
    return lax.broadcasted_iota(jnp.int32, shape, axis)


def dot(left, right, dims):
    return lax.dot_general(left, right, dims, preferred_element_type=jnp.float32)


def hot(mask):
    return jnp.where(mask, 1.0, 0.0).astype(jnp.bfloat16)


def slots_of(bucket, upper, buckets, capacity):
    owner_id = iota((buckets, bucket.shape[1]), 0)
    marked = jnp.where(bucket == owner_id, 1.0, 0.0)
    counted = dot(marked.astype(jnp.bfloat16), upper, NN)
    offset = (owner_id * capacity - 1).astype(jnp.float32)
    return jnp.sum(marked * (counted + offset), axis=0, keepdims=True).astype(jnp.int32)


def split_values(wanted):
    which = iota((16, wanted.shape[1]), 0)
    values = jnp.where(which == 0, wanted >> 6, jnp.where(which == 1, wanted & 63, 0))
    return values.astype(jnp.float32).astype(jnp.bfloat16)


def listed(slot, values, first, width):
    picked = hot(slot == iota((width, slot.shape[1]), 0) + first)
    found = dot(values, picked, NT)
    return (found[0:1] * 64.0 + found[1:2]).astype(jnp.int32)


def front_kernel(
    bra_bucket, bra_wanted, ket_bucket, ket_wanted, table_ref,
    bra_slot, ket_slot, ket_asked, got_out, later_out,
    asked, heard, answer, got, ask_send, ask_recv, ans_send, ans_recv,
    *, peers, cap_bra, kets, cap_ket,
):
    me = lax.axis_index("bra")
    barrier = pltpu.get_barrier_semaphore()
    for k in range(1, peers):
        pl.semaphore_signal(
            barrier, inc=1, device_id={"bra": lax.rem(me + k, peers)},
            device_id_type=pl.DeviceIdType.MESH,
        )
    items = bra_bucket.shape[1]
    width = asked.shape[2]
    blocks = table_ref.shape[0]
    upper = hot(iota((items, items), 0) <= iota((items, items), 1))
    slot = slots_of(bra_bucket[...], upper, 2 * peers, cap_bra)
    slot_k = slots_of(ket_bucket[...], upper, 2 * kets, cap_ket)
    bra_slot[...] = slot
    ket_slot[...] = slot_k
    values = split_values(bra_wanted[...])

    def ask_list(p, carry):
        ids = listed(slot, values, p * (2 * cap_bra), width)
        asked[p] = jnp.broadcast_to(ids, asked.shape[1:])
        return carry

    lax.fori_loop(0, peers, ask_list, 0)

    def ask(k):
        peer = lax.rem(me + k, peers)
        return pltpu.make_async_remote_copy(
            src_ref=asked.at[peer], dst_ref=heard.at[me],
            send_sem=ask_send.at[k], recv_sem=ask_recv.at[k],
            device_id={"bra": peer}, device_id_type=pl.DeviceIdType.MESH,
        )

    def give(k):
        peer = lax.rem(me + peers - k, peers)
        return pltpu.make_async_remote_copy(
            src_ref=answer.at[peer], dst_ref=got.at[me],
            send_sem=ans_send.at[k], recv_sem=ans_recv.at[k],
            device_id={"bra": peer}, device_id_type=pl.DeviceIdType.MESH,
        )

    def serve(ids, which):
        spread = jnp.broadcast_to(ids[0:1], (128, width)).T
        spread = spread[which * cap_bra : (which + 1) * cap_bra]
        spread = jnp.concatenate([spread] * (blocks // 128), axis=1)
        picked = hot(spread == iota((cap_bra, blocks), 1))
        return dot(picked, table_ref[...], NN).astype(jnp.bfloat16)

    pl.semaphore_wait(barrier, peers - 1)

    def send_ask(k, carry):
        ask(k).start()
        return carry

    lax.fori_loop(1, peers, send_ask, 0)
    got[me] = serve(asked[me], 0)
    later_out[me] = serve(asked[me], 1)

    def reply(k, carry):
        ask(k).wait_recv()
        peer = lax.rem(me + peers - k, peers)
        answer[peer] = serve(heard[peer], 0)
        give(k).start()
        return carry

    lax.fori_loop(1, peers, reply, 0)

    def reply_later(k, carry):
        peer = lax.rem(me + peers - k, peers)
        later_out[peer] = serve(heard[peer], 1)
        return carry

    lax.fori_loop(1, peers, reply_later, 0)
    values_k = split_values(ket_wanted[...])
    part = 256

    def place_list(k, carry):
        first = pl.multiple_of(k * part, part)
        ket_asked[:, pl.ds(first, part)] = listed(slot_k, values_k, first, part)
        return carry

    lax.fori_loop(0, ket_asked.shape[1] // part, place_list, 0)

    def finish(k, carry):
        ask(k).wait_send()
        give(k).wait_send()
        give(k).wait_recv()
        return carry

    lax.fori_loop(1, peers, finish, 0)
    got_out[...] = got[...]


def front(bra_bucket, bra_wanted, ket_bucket, ket_wanted, table, peers, cap_bra, kets, cap_ket):
    items = bra_bucket.shape[1]
    width = -(-2 * cap_bra // 128) * 128
    size = table.shape[1]
    blocks = (peers, cap_bra, size)
    return pl.pallas_call(
        functools.partial(
            front_kernel, peers=peers, cap_bra=cap_bra, kets=kets, cap_ket=cap_ket
        ),
        out_shape=[
            jax.ShapeDtypeStruct((1, items), jnp.int32),
            jax.ShapeDtypeStruct((1, items), jnp.int32),
            jax.ShapeDtypeStruct((1, 2 * kets * cap_ket), jnp.int32),
            jax.ShapeDtypeStruct(blocks, jnp.bfloat16),
            jax.ShapeDtypeStruct(blocks, jnp.bfloat16),
        ],
        in_specs=[VMEM] * 5,
        out_specs=[VMEM] * 5,
        scratch_shapes=[
            pltpu.VMEM((peers, 8, width), jnp.int32),
            pltpu.VMEM((peers, 8, width), jnp.int32),
            pltpu.VMEM(blocks, jnp.bfloat16),
            pltpu.VMEM(blocks, jnp.bfloat16),
        ]
        + [pltpu.SemaphoreType.DMA((peers,))] * 4,
        compiler_params=pltpu.CompilerParams(
            vmem_limit_bytes=48 * 1024 * 1024, collective_id=0, has_side_effects=True
        ),
        name="front",
    )(bra_bucket, bra_wanted, ket_bucket, ket_wanted, table)


def pair_rows(slow_ref, slow, fast):
    funcs = fast.shape[0]
    parts = []
    for at in range(funcs):
        row = jnp.broadcast_to(slow_ref[slow, at : at + 1, :], fast.shape).astype(jnp.bfloat16)
        parts.append(row * fast)
    return jnp.concatenate(parts, axis=0)


def task_kernel(
    tasks_ref, slots_ref, places_ref, fac_ref, got_ref, ids_ref, out_ref,
    fac32, got32, dens, spread, dens_cd, partial, coulomb, routed,
    raw_a, raw_b, tile_a, tile_b, unroll,
):
    shells, funcs, terms = fac_ref.shape
    size = funcs * funcs
    count = spread.shape[1]
    raws, tiles = (raw_a, raw_b), (tile_a, tile_b)
    fac32[...] = fac_ref[...].astype(jnp.float32)
    got32[...] = got_ref[...].astype(jnp.float32)

    def gather(t, carry):
        for side in range(2):
            dens[side, pl.ds(t, 1), :] = got32[pl.ds(slots_ref[2 * t + side], 1), :]
        return carry

    lax.fori_loop(0, count, gather, 0, unroll=8)
    row, col = iota((size, size), 0), iota((size, size), 1)
    row_hi, row_lo, col_hi, col_lo = row // funcs, row % funcs, col // funcs, col % funcs
    swap = hot((row_hi == col_lo) & (row_lo == col_hi))
    dens_cd[...] = dot(dens[0].astype(jnp.bfloat16), swap, NN)
    dens_jd = dens[1].astype(jnp.bfloat16)

    def spread_one(f, carry):
        spread[f] = dot(dens_jd, hot((row_hi == col_lo) & (row_lo == f)), NN)
        return carry

    lax.fori_loop(0, funcs, spread_one, 0, unroll=8)

    def form(t, raw_ref, k):
        shell_i, shell_j = tasks_ref[4 * t], tasks_ref[4 * t + 1]
        shell_c, shell_d = tasks_ref[4 * t + 2], tasks_ref[4 * t + 3]
        ket = pair_rows(fac32, shell_d, fac_ref[shell_c])
        bra = pair_rows(fac32, shell_i, fac_ref[shell_j])
        raw_ref[k] = dot(ket, bra, NT).astype(raw_ref.dtype)

    def bound(t, raw_ref, tile_ref, k):
        total = None
        for f in range(0, funcs, 2):
            terms_of = []
            for g in (f, f + 1):
                rows = slice(g * funcs, (g + 1) * funcs)
                raw = raw_ref[k, rows, :]
                tile = raw * lax.rsqrt(raw * raw + jnp.ones_like(raw))
                tile_ref[k, rows, :] = tile
                held = jnp.broadcast_to(spread[g, pl.ds(t, 1), :], (funcs, size))
                terms_of.append(tile * held.astype(tile.dtype))
            term = (terms_of[0] + terms_of[1]).astype(jnp.float32)
            total = term if total is None else total + term
        place = pl.ds(pl.multiple_of(t * funcs, funcs), funcs)
        for lane in range(size // 128):
            partial[lane, place, :] = total[:, lane * 128 : (lane + 1) * 128]

    def contract(t, tile_ref, k):
        weights = jnp.broadcast_to(dens_cd[pl.ds(t, 1), :], (16, size)).astype(jnp.bfloat16)
        summed = dot(weights, tile_ref[k], NN)
        coulomb[pl.ds(t, 1), :] = summed[0:1]

    batches = count // unroll

    def first_of(batch):
        return jnp.clip(batch, 0, batches - 1) * unroll

    def steps(pair, carry):
        for odd in range(2):
            batch = 2 * pair + odd
            here, there = (0, 1) if odd == 0 else (1, 0)
            for k in range(unroll):
                contract(first_of(batch - 2) + k, tiles[here], k)
                bound(first_of(batch - 1) + k, raws[there], tiles[there], k)
                form(first_of(batch) + k, raws[here], k)
        return carry

    lax.fori_loop(0, (batches + 2) // 2, steps, 0)

    dens[0] = coulomb[...] * tile_scale
    dens[1] = jnp.zeros((count, size), jnp.float32)

    def fold(e, carry):
        picked = pl.ds(e, count, stride=funcs)
        rows = [partial[lane, picked, :] for lane in range(size // 128)]
        rows = jnp.concatenate(rows, axis=1).astype(jnp.bfloat16)
        dens[1] += dot(rows, hot((row_hi == col_hi) & (col_lo == e)), NN)
        return carry

    lax.fori_loop(0, funcs, fold, 0, unroll=8)
    dens[1] = dens[1] * (-0.5 * tile_scale)
    routed[...] = jnp.zeros_like(routed)
    owners = ids_ref.shape[0] // 2
    stride = routed.shape[0] // owners
    for owner in range(owners):
        last = (owner + 1) * stride - id_rows
        routed[last : last + 2, :] = ids_ref[2 * owner : 2 * owner + 2, :]

    def route(t, carry):
        for side in range(2):
            routed[pl.ds(places_ref[2 * t + side], 1), :] = dens[side, pl.ds(t, 1), :]
        return carry

    lax.fori_loop(0, count, route, 0, unroll=8)
    out_ref[...] = routed[...].astype(jnp.bfloat16)


def run_tasks(tasks, slots, places, factors, got, ids, out_rows, unroll):
    count = tasks.shape[0] // 4
    shells, funcs, terms = factors.shape
    size = funcs * funcs
    f32 = jnp.float32
    return pl.pallas_call(
        functools.partial(task_kernel, unroll=unroll),
        out_shape=jax.ShapeDtypeStruct((out_rows, size), jnp.bfloat16),
        in_specs=[SMEM, SMEM, SMEM, VMEM, VMEM, VMEM],
        out_specs=VMEM,
        scratch_shapes=[
            pltpu.VMEM((shells, funcs, terms), f32),
            pltpu.VMEM(got.shape, f32),
            pltpu.VMEM((2, count, size), f32),
            pltpu.VMEM((funcs, count, size), f32),
            pltpu.VMEM((count, size), f32),
            pltpu.VMEM((size // 128, count * funcs, 128), f32),
            pltpu.VMEM((count, size), f32),
            pltpu.VMEM((out_rows, size), f32),
        ]
        + [pltpu.VMEM((unroll, size, size), jnp.bfloat16)] * 4,
        compiler_params=PARAMS,
        cost_estimate=pl.CostEstimate(
            flops=16 * count * size * size * terms,
            bytes_accessed=2 * shells * funcs * terms,
            transcendentals=count * size * size,
        ),
        name="tasks",
    )(tasks, slots, places, factors, got, ids)


def sum_kernel(block_a, own_b, out_ref, got, sent, arrived, *, sources):
    me = lax.axis_index("ket")
    barrier = pltpu.get_barrier_semaphore()
    for k in range(1, sources):
        pl.semaphore_signal(
            barrier, inc=1, device_id={"ket": lax.rem(me + k, sources)},
            device_id_type=pl.DeviceIdType.MESH,
        )
    pl.semaphore_wait(barrier, sources - 1)
    copies = []
    for k in range(1, sources):
        peer = lax.rem(me + k, sources)
        copies.append(
            pltpu.make_async_remote_copy(
                src_ref=own_b.at[peer], dst_ref=got.at[k],
                send_sem=sent.at[k], recv_sem=arrived.at[k],
                device_id={"ket": peer}, device_id_type=pl.DeviceIdType.MESH,
            )
        )
        copies[-1].start()
    rows = 128
    stride = block_a.shape[1]

    def add(pairs, start):
        def chunk(at, carry):
            first = pl.multiple_of(at * rows, rows)
            here = (iota((rows, stride), 0) + first).astype(jnp.float32)
            place = pl.ds(first, rows)
            total = None if start else out_ref[place, :]
            for read in pairs:
                held = read()
                ids = held[stride - id_rows :, :].astype(jnp.float32)
                index = (ids[0:1] * 64.0 + ids[1:2])[:, :stride]
                term = dot(hot(jnp.broadcast_to(index, here.shape) == here), held, NN)
                total = term if total is None else total + term
            out_ref[place, :] = total
            return carry

        lax.fori_loop(0, out_ref.shape[0] // rows, chunk, 0)

    early = [functools.partial(lambda k: block_a[k], k) for k in range(sources)]
    add(early + [lambda: own_b[me]], True)
    for copy in copies:
        copy.wait()
    add([functools.partial(lambda k: got[k], k) for k in range(1, sources)], False)


def sum_blocks(block_a, own_b, total):
    sources, stride, size = block_a.shape
    return pl.pallas_call(
        functools.partial(sum_kernel, sources=sources),
        out_shape=jax.ShapeDtypeStruct((total, size), jnp.float32),
        in_specs=[VMEM, VMEM],
        out_specs=VMEM,
        scratch_shapes=[
            pltpu.VMEM((sources, stride, size), jnp.bfloat16),
            pltpu.SemaphoreType.DMA((sources,)),
            pltpu.SemaphoreType.DMA((sources,)),
        ],
        compiler_params=pltpu.CompilerParams(
            vmem_limit_bytes=48 * 1024 * 1024, collective_id=1, has_side_effects=True
        ),
        name="sum_blocks",
    )(block_a, own_b)


def trade(array, axis):
    return lax.all_to_all(array, axis, split_axis=0, concat_axis=0, tiled=True)


def body(quartet_tasks, factors, density):
    quartets = quartet_tasks.reshape(-1, 4)
    task_count = quartets.shape[0]
    half = task_count // 2
    bra_count = lax.axis_size("bra")
    ket_count = lax.axis_size("ket")
    rows_per_device, cols_dev, size = (density.shape[0], density.shape[1], density.shape[3])
    table = density.reshape(rows_per_device * cols_dev, size)
    shell_i, shell_j, shell_c, shell_d = (quartets[:, k] for k in range(4))

    cap_bra = 3 * task_count // bra_count
    cap_ket = 5 * task_count // (4 * ket_count)
    half_of = jnp.arange(2 * task_count, dtype=jnp.int32) // task_count
    wanted_shell = jnp.stack([shell_c, shell_j], axis=1).reshape(-1)
    wanted = wanted_shell % rows_per_device * cols_dev + jnp.repeat(shell_d // ket_count, 2)
    bra_bucket = wanted_shell // rows_per_device * 2 + half_of
    target = jnp.stack([shell_j, shell_c], axis=1).reshape(-1)
    position = jnp.repeat(shell_i % rows_per_device, 2) * cols_dev + target // ket_count
    ket_bucket = target % ket_count * 2 + half_of
    slot_bra, slot_ket, asked_ket, first_got, later = front(
        bra_bucket[None], wanted[None], ket_bucket[None], position[None], table,
        bra_count, cap_bra, ket_count, cap_ket,
    )
    slots = (slot_bra, slot_ket)

    def per_half(slot, capacity, stride, which):
        bucket, place = slot // capacity, slot % capacity
        local = bucket // 2 * stride + place
        return local[which * task_count : (which + 1) * task_count]

    stride = cap_ket + id_rows
    ids = asked_ket.reshape(ket_count, 2, cap_ket)
    ids = jnp.stack([ids >> 6, ids & 63], axis=2).astype(jnp.float32)
    ids = jnp.pad(ids, ((0, 0), (0, 0), (0, 0), (0, size - cap_ket)), constant_values=-1.0)

    results = []
    for which in range(2):
        got = first_got if which == 0 else trade(later, "bra")
        outgoing = run_tasks(
            quartets[which * half : (which + 1) * half].reshape(-1),
            per_half(slots[0].reshape(-1), cap_bra, cap_bra, which),
            per_half(slots[1].reshape(-1), cap_ket, stride, which),
            factors,
            got.reshape(-1, size),
            ids[:, which].reshape(-1, size),
            ket_count * stride,
            4,
        )
        outgoing = outgoing.reshape(ket_count, stride, size)
        results.append(trade(outgoing, "ket") if which == 0 else outgoing)
    fock = sum_blocks(results[0], results[1], rows_per_device * cols_dev)
    return fock.reshape(rows_per_device, cols_dev, 1, size)


def solution(mesh):
    placed = (P("bra", "ket", None, None), P(), P("bra", None, "ket", None))
    return jax.shard_map(
        body, mesh=mesh, in_specs=placed, out_specs=P("bra", None, "ket", None), check_vma=False
    )
```
